32 devices in a mesh: ctx: 8 (over z, core), hd: 4 (over y, x).
Axes of the slice: x: 2, y: 2, z: 4, core: 2. Of those that a mesh axis runs over, the one named last changes fastest.
Arguments:
- layer_input_rows: bfloat16 [4096, 1024], P(('ctx', 'hd')), may hold values from -6 to 6
- first_layer_values: bfloat16 [4096, 1024], P(('ctx', 'hd')), may hold values from -6 to 6
- cotangent: bfloat16 [4096, 1024], P(('ctx', 'hd')), may hold values from -6 to 6
- projection_weights: bfloat16 [3, 1024, 1024], P(None, 'ctx', 'hd'), may hold values from -0.1875 to 0.1875
- output_weight: bfloat16 [1024, 1024], P('hd', 'ctx'), may hold values from -0.1875 to 0.1875
- lowrank_in_factors: bfloat16 [1024, 288], P('ctx'), may hold values from -0.1875 to 0.1875
- lowrank_out_factors: bfloat16 [288, 1024], P(None, 'ctx'), may hold values from -0.75 to 0.75
- shift_mix_factors: bfloat16 [7, 1024], P(None, 'ctx'), may hold values from 0 to 1
- parameter_lines: bfloat16 [12, 1024], P(None, 'ctx'), may hold values from -16 to 2, as said below
- channel_key_weight: bfloat16 [1024, 4096], P('ctx', 'hd'), may hold values from -0.1875 to 0.1875
- channel_value_weight: bfloat16 [4096, 1024], P('hd', 'ctx'), may hold values from -0.09375 to 0.09375
Outputs:
- layer_output: bfloat16 [4096, 1024], P(('ctx', 'hd'))
- grad_input: float32 [4096, 1024], P(('ctx', 'hd'))
- grad_value_first: float32 [4096, 1024], P(('ctx', 'hd'))
- grad_proj_weight: float32 [3, 1024, 1024], P(None, 'ctx', 'hd')
- grad_out_weight: float32 [1024, 1024], P('hd', 'ctx')
- grad_lora_in: float32 [1024, 288], P(('ctx', 'hd'))
- grad_lora_out: float32 [288, 1024], P(None, ('ctx', 'hd'))
- grad_mix_coef: float32 [6, 1024], P(None, ('ctx', 'hd'))
- grad_vectors: float32 [12, 1024], P(None, ('ctx', 'hd'))
- grad_ffn_key: float32 [1024, 4096], P('ctx', 'hd')
- grad_ffn_value: float32 [4096, 1024], P('hd', 'ctx')
- grad_decay_mix: float32 [1024], P(('ctx', 'hd'))
The draws below stay inside these ranges and needn't reach their ends.
Inputs may be any that keep to these rules, and one draw needn't show every extreme that they name: `parameter_lines`: rows 0, 2, 4, 9, 10 lie in 0.5 to 1.5; rows 1, 3, 5 in -0.5 to 0.5; rows 7 and 8 in -2 to 2; row 11 in -1 to 1; row 6 is negative.
All inputs are finite; a program needn't handle non-finite values.
Results may differ from the reference program's by a relative error of at most 0.023.
Values may be sent and summed in bfloat16 or wider, within the bound.
No kernel may reach another device: no remote copies, remote signals or barrier semaphores. Data moves between devices by JAX's collectives and lax.ppermute only.
A program may use at most 320 MiB of HBM per device.

```python
import math
import jax
import jax.numpy as jnp
from jax import lax

EMBEDDING_SIZE = 1024
ATTENDER_TOTAL = 16
ATTENDER_SIZE = 64
FF = 4096
DECAY_LOWRANK = 64
RA = 64
RV = 32
LOWRANK_COLUMNS = 288
SEQUENCE_LENGTH = 4096


def draw_parameter_lines(key, part):
    pieces = jax.random.split(jax.random.fold_in(key, 7), 2)
    uniform_draw = jax.random.uniform(pieces[0], (12, EMBEDDING_SIZE), jnp.float32)
    low_end = math.log(30.0)
    high_end = math.log(4.0 * SEQUENCE_LENGTH)
    log_life = low_end + (high_end - low_end) * jax.random.uniform(pieces[1], (EMBEDDING_SIZE,), jnp.float32)
    shift_offset = -jnp.log(jnp.expm1(log_life - 0.5))
    gain_rows = 0.5 + uniform_draw
    bias_rows = uniform_draw - 0.5
    wide_rows = 4.0 * uniform_draw - 2.0
    signed_rows = 2.0 * uniform_draw - 1.0
    stacked_rows = [gain_rows[0], bias_rows[1], gain_rows[2], bias_rows[3], gain_rows[4], bias_rows[5], shift_offset, wide_rows[7], wide_rows[8], gain_rows[9], gain_rows[10], signed_rows[11]]
    return jnp.stack(stacked_rows).astype(jnp.bfloat16)


def levels(stream_key, shape, cuts, smallest, largest):
    def one(axis_at, shards_of):
        draws = jax.random.uniform(jax.random.fold_in(jax.random.fold_in(stream_key, 6), axis_at), (shards_of,), jnp.float32, smallest / len(cuts), largest / len(cuts))
        return jnp.repeat(jnp.exp(draws), shape[axis_at] // shards_of).reshape((-1,) + (1,) * (len(shape) - axis_at - 1))

    loudness = one(*cuts[0])
    for cut in cuts[1:]:
        loudness = loudness * one(*cut)
    return loudness


def noise(stream_key, dims, width, limit, cuts=(), dtype=jnp.bfloat16):
    level = levels(stream_key, dims, cuts, -0.22, 0.18) if cuts else 1.0
    drawn = jax.random.normal(stream_key, dims, jnp.float32) * width * level
    return jnp.minimum(jnp.maximum(drawn, -limit), limit).astype(dtype)


def setup_inputs(seed: int = 0) -> dict:
    streams_of = jax.random.split(jax.random.key(seed), 12)
    layer_input_rows = noise(streams_of[0], (SEQUENCE_LENGTH, EMBEDDING_SIZE), 1.0, 6.0, ((0, 32),))
    first_layer_values = noise(streams_of[1], (SEQUENCE_LENGTH, EMBEDDING_SIZE), 1.0, 6.0, ((0, 32),))
    cotangent = noise(streams_of[2], (SEQUENCE_LENGTH, EMBEDDING_SIZE), 1.0, 6.0, ((0, 32),))
    projection_weights = noise(streams_of[3], (3, EMBEDDING_SIZE, EMBEDDING_SIZE), EMBEDDING_SIZE ** -0.5, 0.1875, ((1, 8), (2, 4)))
    output_weight = noise(streams_of[4], (EMBEDDING_SIZE, EMBEDDING_SIZE), EMBEDDING_SIZE ** -0.5, 0.1875, ((0, 4), (1, 8)))
    lowrank_in_factors = noise(streams_of[5], (EMBEDDING_SIZE, LOWRANK_COLUMNS), EMBEDDING_SIZE ** -0.5, 0.1875, ((0, 8),))
    lowrank_out_factors = noise(streams_of[6], (LOWRANK_COLUMNS, EMBEDDING_SIZE), DECAY_LOWRANK ** -0.5, 0.75, ((1, 8),))
    shift_mix_factors = jnp.clip(1.0 * jax.random.uniform(streams_of[7], (7, EMBEDDING_SIZE), jnp.float32) ** levels(streams_of[7], (7, EMBEDDING_SIZE), ((1, 8),), -0.2, 0.2), 0.0, 1.0).astype(jnp.bfloat16)
    parameter_lines = draw_parameter_lines(jax.random.fold_in(streams_of[11], 71), 0)
    channel_key_weight = noise(streams_of[9], (EMBEDDING_SIZE, FF), EMBEDDING_SIZE ** -0.5, 0.1875, ((0, 8), (1, 4)))
    channel_value_weight = noise(streams_of[10], (FF, EMBEDDING_SIZE), FF ** -0.5, 0.09375, ((0, 4), (1, 8)))
    return dict(layer_input_rows=layer_input_rows, first_layer_values=first_layer_values, cotangent=cotangent, projection_weights=projection_weights, output_weight=output_weight, lowrank_in_factors=lowrank_in_factors, lowrank_out_factors=lowrank_out_factors, shift_mix_factors=shift_mix_factors, parameter_lines=parameter_lines, channel_key_weight=channel_key_weight, channel_value_weight=channel_value_weight)


HIGH = lax.Precision.HIGHEST
scan_rows = 256

@jax.custom_vjp
def low(v):
    return lax.optimization_barrier(v.astype(jnp.bfloat16)).astype(jnp.float32)

@jax.custom_vjp
def low_back(v):
    return v

def low_keep(v):
    return (low(v), None)

def low_pass(kept, grad):
    return (grad,)

def back_keep(v):
    return (v, None)

def back_low(kept, grad):
    return (low(grad),)
low.defvjp(low_keep, low_pass)
low_back.defvjp(back_keep, back_low)

def matrix_multiply(left_side, right_side):
    return jnp.dot(left_side, right_side, precision=HIGH, preferred_element_type=jnp.float32)

def layer_norm(hidden, gain_row, bias_row):
    row_mean = lax.optimization_barrier(jnp.mean(hidden, -1, keepdims=True))
    centered = hidden - row_mean
    inv_std = lax.rsqrt(lax.optimization_barrier(jnp.mean(centered * centered, -1, keepdims=True)) + 1e-05)
    return centered * inv_std * gain_row + bias_row

def shifted(hidden):
    return jnp.concatenate([jnp.zeros_like(hidden[:1]), hidden[:-1]], 0)

def as_heads(input_tensor):
    return input_tensor.reshape(SEQUENCE_LENGTH, ATTENDER_TOTAL, ATTENDER_SIZE)

def recurrence(receptance, log_decay_value, key_part, value_part, removal, learning_rate):
    decay_rate = jnp.exp(log_decay_value)
    beside = removal * learning_rate

    def token_step(carried, token_items):
        recept_t, decay_t, key_t, value_t, removal_t, beside_t = token_items
        along_t = jnp.einsum('hvk,hk->hv', carried, -removal_t, precision=HIGH)
        carried = carried * decay_t[:, None, :] + along_t[:, :, None] * beside_t[:, None, :] + value_t[:, :, None] * key_t[:, None, :]
        return (carried, jnp.einsum('hvk,hk->hv', carried, recept_t, precision=HIGH))

    def block_step(carried, block_items):
        return lax.scan(token_step, carried, block_items)
    stacked = tuple((input_tensor.reshape(SEQUENCE_LENGTH // scan_rows, scan_rows, ATTENDER_TOTAL, ATTENDER_SIZE) for input_tensor in (receptance, decay_rate, key_part, value_part, removal, beside)))
    zero_state = jnp.zeros((ATTENDER_TOTAL, ATTENDER_SIZE, ATTENDER_SIZE), jnp.float32)
    final_state, outputs = lax.scan(jax.checkpoint(block_step), zero_state, stacked)
    return outputs.reshape(SEQUENCE_LENGTH, ATTENDER_TOTAL, ATTENDER_SIZE)

def forward_pass(residual_input, initial_values, projection_stack, output_projection, lowrank_first_factor, lowrank_second_factor, token_mixing, printed_strings, key_projection, value_projection):
    normed = layer_norm(residual_input, printed_strings[0], printed_strings[1])
    delta_one = shifted(normed) - normed
    mixed = [low(normed + delta_one * token_mixing[index_mix]) for index_mix in range(6)]
    receptance = matrix_multiply(mixed[0], projection_stack[0])
    key_proj = low_back(matrix_multiply(mixed[2], projection_stack[1]))
    value_proj = low_back(matrix_multiply(mixed[3], projection_stack[2]))
    decay_boundary = DECAY_LOWRANK
    rate_boundary = DECAY_LOWRANK + RA
    value_boundary = DECAY_LOWRANK + RA + RV
    hidden_decay = low(jnp.tanh(low_back(matrix_multiply(mixed[1], lowrank_first_factor[:, :decay_boundary]))))
    hidden_rate = low(low_back(matrix_multiply(mixed[4], lowrank_first_factor[:, decay_boundary:rate_boundary])))
    hidden_value = low(low_back(matrix_multiply(mixed[3], lowrank_first_factor[:, rate_boundary:value_boundary])))
    hidden_gate = low(jax.nn.sigmoid(low_back(matrix_multiply(mixed[5], lowrank_first_factor[:, value_boundary:]))))
    lowrank_decay = low_back(matrix_multiply(hidden_decay, lowrank_second_factor[:decay_boundary]))
    lowrank_rate = low_back(matrix_multiply(hidden_rate, lowrank_second_factor[decay_boundary:rate_boundary]))
    lowrank_value = low_back(matrix_multiply(hidden_value, lowrank_second_factor[rate_boundary:value_boundary]))
    gate_sent = low(low_back(matrix_multiply(hidden_gate, lowrank_second_factor[value_boundary:])))
    decay_sent = low(low_back(-jnp.exp(-jax.nn.softplus(-(printed_strings[6] + lowrank_decay)) - 0.5)))
    rate_sent = low(low_back(jax.nn.sigmoid(printed_strings[7] + lowrank_rate)))
    mix_sent = low(low_back(jax.nn.sigmoid(printed_strings[8] + lowrank_value)))
    key_raw = as_heads(key_proj * printed_strings[9])
    removal = key_raw * lax.rsqrt(lax.optimization_barrier(jnp.mean(key_raw * key_raw, -1, keepdims=True)) + 1e-05) / math.sqrt(ATTENDER_SIZE)
    key_mod = key_proj * (1.0 + (rate_sent - 1.0) * printed_strings[10])
    value_mod = value_proj + (initial_values - value_proj) * mix_sent
    carried_acceptance = as_heads(low(low_back(receptance)))
    carried_lookup = as_heads(low(low_back(key_mod)))
    carried_content = as_heads(low(low_back(value_mod)))
    sent_removal = low(low_back(removal))
    head_y = recurrence(carried_acceptance, as_heads(decay_sent), carried_lookup, carried_content, sent_removal, as_heads(rate_sent))
    head_mean = lax.optimization_barrier(jnp.mean(head_y, -1, keepdims=True))
    centered = head_y - head_mean
    head_inv = lax.rsqrt(lax.optimization_barrier(jnp.mean(centered * centered, -1, keepdims=True)) + 1e-05 * ATTENDER_SIZE)
    standardized = centered * head_inv * printed_strings[2].reshape(ATTENDER_TOTAL, ATTENDER_SIZE) + printed_strings[3].reshape(ATTENDER_TOTAL, ATTENDER_SIZE)
    extra_contribution = lax.optimization_barrier(jnp.sum(carried_acceptance * carried_lookup * printed_strings[11].reshape(ATTENDER_TOTAL, ATTENDER_SIZE), -1, keepdims=True)) * carried_content
    head_out = low(low_back(standardized + extra_contribution)).reshape(SEQUENCE_LENGTH, EMBEDDING_SIZE)
    att_in = low(head_out * gate_sent)
    residual = residual_input + low_back(matrix_multiply(att_in, output_projection))
    normed_two = layer_norm(residual, printed_strings[4], printed_strings[5])
    mixed_ffn = low(normed_two + (shifted(normed_two) - normed_two) * token_mixing[6])
    pre_ffn = low_back(matrix_multiply(mixed_ffn, key_projection))
    squared = low(jnp.square(jax.nn.relu(pre_ffn)))
    return residual + matrix_multiply(squared, value_projection)

def reference(layer_input_rows, first_layer_values, cotangent, projection_weights, output_weight, lowrank_in_factors, lowrank_out_factors, shift_mix_factors, parameter_lines, channel_key_weight, channel_value_weight):
    input_arrays = tuple((input_tensor.astype(jnp.float32) for input_tensor in (layer_input_rows, first_layer_values, projection_weights, output_weight, lowrank_in_factors, lowrank_out_factors, shift_mix_factors, parameter_lines, channel_key_weight, channel_value_weight)))
    result, pullback = jax.vjp(forward_pass, *input_arrays)
    gradients = pullback(cotangent.astype(jnp.float32))
    mixing_gradient = gradients[6]
    other_mixing = jnp.concatenate([mixing_gradient[:1], mixing_gradient[2:]], 0)
    return (result.astype(jnp.bfloat16), gradients[0], gradients[1], gradients[2], gradients[3], gradients[4], gradients[5], other_mixing, gradients[7], gradients[8], gradients[9], mixing_gradient[1])
```

```python
import functools
import math

import jax
import jax.numpy as jnp
from jax import lax
from jax.experimental import pallas as pl
from jax.experimental.pallas import tpu as pltpu
from jax.sharding import PartitionSpec as P

HEAD = 64
DECAY_LOWRANK = 64
RA = 64
RV = 32
CHUNK = 64
BF = jnp.bfloat16
F32 = jnp.float32
HIGH = lax.Precision.HIGHEST
FORMS = {"nn": ((1,), (0,)), "nt": ((1,), (1,)), "tn": ((0,), (0,))}


def product(left, right, form="nn"):
    return lax.dot_general(left, right, (FORMS[form], ((), ())), preferred_element_type=F32)


def mm(left, right, form="nn"):
    return product(left.astype(BF), right.astype(BF), form)


def fine(left, right, form="nn"):
    left_top, right_top = left.astype(BF), right.astype(BF)
    left_rest = (left - left_top.astype(F32)).astype(BF)
    right_rest = (right - right_top.astype(F32)).astype(BF)
    return (
        product(left_top, right_top, form)
        + product(left_top, right_rest, form)
        + product(left_rest, right_top, form)
    )


def exact(left, right, form="nn"):
    return lax.dot_general(
        left, right, (FORMS[form], ((), ())), precision=HIGH, preferred_element_type=F32
    )


def iotas(rows, cols):
    return (
        lax.broadcasted_iota(jnp.int32, (rows, cols), 0),
        lax.broadcasted_iota(jnp.int32, (rows, cols), 1),
    )


def div(value, size):
    return lax.div(value, jnp.int32(size))


def ones_where(condition):
    return jnp.where(condition, 1.0, 0.0)


def heads_mask(heads, rows):
    row, col = iotas(heads * rows, heads * HEAD)
    return ones_where(div(row, rows) == div(col, HEAD))


def spread(rows, mask):
    return jnp.concatenate([rows] * (mask.shape[0] // rows.shape[0]), 0) * mask


def fold(tall, heads):
    step = tall.shape[0] // heads
    total = tall[:step]
    for i in range(1, heads):
        total = total + tall[i * step : (i + 1) * step]
    return total


def causal_masks(heads):
    row, col = iotas(heads * CHUNK, heads * CHUNK)
    return ones_where(row > col), ones_where(row >= col)


def rounded(value):
    return value.astype(BF).astype(F32)


def chunk_factors(r, w, k, kk, a):
    row, col = iotas(CHUNK, CHUNK)
    cum = mm(ones_where(row >= col), w)
    total = cum[CHUNK - 1 :]
    up, down, fade = jnp.exp(cum), jnp.exp(-cum), jnp.exp(total - cum)
    ahead = jnp.exp(cum - w)
    be = kk * a
    return dict(
        up=up,
        down=down,
        fade=fade,
        ahead=ahead,
        decay=jnp.exp(total),
        al=rounded(-kk * ahead),
        rs=rounded(r * up),
        bi=rounded(be * down),
        ki=rounded(k * down),
        bf=rounded(be * fade),
        kf=rounded(k * fade),
    )


def inverse(strict_part):
    size = strict_part.shape[0]
    row, col = iotas(size, size)
    out = ones_where(row == col)
    width = 1
    while width < CHUNK:
        pick = (div(row, 2 * width) == div(col, 2 * width)) & (div(row, width) != div(col, width))
        part = jnp.where(pick, strict_part, 0.0)
        out = out + (part if width == 1 else mm(mm(out, part), out))
        width *= 2
    return out


def forward_kernel(heads, r_ref, w_ref, k_ref, v_ref, kk_ref, a_ref, y_ref, starts_ref, tri_ref, last_ref, state):
    W, HC = heads * HEAD, heads * CHUNK

    @pl.when(pl.program_id(0) == 0)
    def _():
        row, col = iotas(2 * W, W)
        state[...] = ones_where(row == col + W)

    r, w, k, v, kk, a = [
        ref[...].astype(F32) for ref in (r_ref, w_ref, k_ref, v_ref, kk_ref, a_ref)
    ]
    f = chunk_factors(r, w, k, kk, a)
    mask = heads_mask(heads, CHUNK)
    strict, incl = causal_masks(heads)

    def lift(value):
        return spread(value, mask).astype(BF)

    alrs = jnp.concatenate([lift(f["al"]), lift(f["rs"])], 0)
    biki = jnp.concatenate([lift(f["bi"]), lift(f["ki"])], 0)
    scores = product(alrs, biki, "nt")
    tri = inverse(scores[:HC, :HC] * strict).astype(BF)
    vb = lift(v)
    early = state[...]
    starts_ref[0] = early
    tri_ref[0] = tri
    seen = product(alrs, early.astype(BF), "nt")
    given = mm(
        jnp.concatenate([scores[:HC, HC:] * strict, scores[HC:, HC:] * incl], 0), vb
    )
    zero = jnp.zeros((HC, W), F32)
    u = mm(tri, seen[:HC] + jnp.concatenate([given[:HC], zero], 1)).astype(BF)
    y = seen[HC:] + mm(scores[HC:, :HC] * incl, u) + jnp.concatenate([given[HC:], zero], 1)
    y_ref[...] = fold(y, heads)
    late = (
        early * f["decay"]
        + product(u, lift(f["bf"]), "tn")
        + jnp.concatenate([product(vb, lift(f["kf"]), "tn"), jnp.zeros((W, W), F32)], 0)
    )
    state[...] = late

    @pl.when(pl.program_id(0) == pl.num_programs(0) - 1)
    def _():
        def narrow(block_diagonal):
            total = block_diagonal[:, :HEAD]
            for i in range(1, heads):
                total = total + block_diagonal[:, i * HEAD : (i + 1) * HEAD]
            return total

        last_ref[...] = jnp.concatenate([narrow(late[:W]), narrow(late[W:])], 1)


def chunk_spec(width, count, reverse):
    if reverse:
        return pl.BlockSpec((CHUNK, width), lambda i: (count - 1 - i, 0))
    return pl.BlockSpec((CHUNK, width), lambda i: (i, 0))


def stack_spec(shape, count, reverse):
    if reverse:
        return pl.BlockSpec((1,) + shape, lambda i: (count - 1 - i, 0, 0))
    return pl.BlockSpec((1,) + shape, lambda i: (i, 0, 0))


def whole_spec(shape):
    return pl.BlockSpec(shape, lambda i: (0,) * len(shape))


def run_forward(r, w, k, v, kk, a):
    span, W = r.shape
    heads, count = W // HEAD, span // CHUNK
    HC = heads * CHUNK
    return pl.pallas_call(
        functools.partial(forward_kernel, heads),
        grid=(count,),
        in_specs=[chunk_spec(W, count, False)] * 6,
        out_specs=[
            chunk_spec(2 * W, count, False),
            stack_spec((2 * W, W), count, False),
            stack_spec((HC, HC), count, False),
            whole_spec((W, 2 * HEAD)),
        ],
        out_shape=[
            jax.ShapeDtypeStruct((span, 2 * W), F32),
            jax.ShapeDtypeStruct((count, 2 * W, W), F32),
            jax.ShapeDtypeStruct((count, HC, HC), BF),
            jax.ShapeDtypeStruct((W, 2 * HEAD), F32),
        ],
        scratch_shapes=[pltpu.VMEM((2 * W, W), F32)],
        compiler_params=pltpu.CompilerParams(vmem_limit_bytes=48 * 1024 * 1024),
        cost_estimate=pl.CostEstimate(
            flops=count * 27 * 2 * HC * HC * W, bytes_accessed=count * 2**20, transcendentals=0
        ),
        name="recurrence_forward",
    )(r, w, k, v, kk, a)


def shift_up(value, last_row):
    size = value.shape[0]
    row = lax.broadcasted_iota(jnp.int32, value.shape, 0)
    return jnp.where(row == size - 1, last_row, pltpu.roll(value, size - 1, 0))


def backward_kernel(heads, per_block, *refs):
    chunks, wholes, outs, scratches = refs[:19], refs[19:25], refs[25:33], refs[33:]
    adjoint, behind = scratches
    (
        r_ref,
        w_ref,
        k_ref,
        v_ref,
        kk_ref,
        a_ref,
        gate_ref,
        first_ref,
        seed_in_ref,
        dy_ref,
        key_ref,
        value_ref,
        decay_slope_ref,
        rate_slope_ref,
        gate_slope_ref,
        out_grad_ref,
        delta_ref,
        starts_ref,
        tri_ref,
    ) = chunks
    enter_ref, end_ref, lines_ref, blocks_ref, weight_ref, mix_ref = wholes
    receptance_out, key_out, value_out, lora_out, token_out, sums_ref, back_ref, mix_sums_ref = outs
    W, HC = heads * HEAD, heads * CHUNK

    @pl.when(pl.program_id(0) == 0)
    def _():
        adjoint[...] = end_ref[...]
        sums_ref[...] = jnp.zeros(sums_ref.shape, F32)
        mix_sums_ref[...] = jnp.zeros(mix_sums_ref.shape, F32)
        behind[...] = jnp.zeros(behind.shape, F32)

    r, w, k, v, kk, a, mix, first, dout = [
        ref[...].astype(F32)
        for ref in (
            r_ref, w_ref, k_ref, v_ref, kk_ref, a_ref, gate_ref, first_ref, seed_in_ref
        )
    ]
    G = adjoint[...]
    starts = starts_ref[0]
    S = starts[:W] + mm(enter_ref[...], starts[W:])
    tri = tri_ref[0]
    f = chunk_factors(r, w, k, kk, a)
    mask = heads_mask(heads, CHUNK)
    strict, incl = causal_masks(heads)
    half = jnp.concatenate([strict, incl], 0)
    both = jnp.concatenate([half, half], 1)

    def lift(value):
        return spread(value, mask).astype(BF)

    alrs = jnp.concatenate([lift(f["al"]), lift(f["rs"])], 0)
    biki = jnp.concatenate([lift(f["bi"]), lift(f["ki"])], 0)
    bef, kef, vb, dyb = lift(f["bf"]), lift(f["kf"]), lift(v), lift(dy_ref[...])
    sb, gb = S.astype(BF), G.astype(BF)
    scores = (product(alrs, biki, "nt") * both).astype(BF)
    rhs = product(alrs[:HC], sb, "nt") + product(scores[:HC, HC:], vb)
    u = mm(tri, rhs).astype(BF)
    du = product(scores[HC:, :HC], dyb, "tn") + product(bef, gb, "nt")
    drhs = mm(tri, du, "tn").astype(BF)
    dd = jnp.concatenate([drhs, dyb], 0)
    uv = jnp.concatenate([u, vb], 0)
    dscores = (product(dd, uv, "nt") * both).astype(BF)
    dalrs = product(dd, sb) + product(dscores, biki)
    dbiki = product(dscores, alrs, "tn")
    dv = fold(product(scores[:, HC:], dd, "tn") + product(kef, gb, "nt"), heads)
    adjoint[...] = G * f["decay"] + product(dd, alrs, "tn")
    dbk = product(uv, gb)
    dal, drs = fold(dalrs[:HC], heads), fold(dalrs[HC:], heads)
    dbi, dki = fold(dbiki[:HC], heads), fold(dbiki[HC:], heads)
    dbf, dkf = fold(dbk[:HC], heads), fold(dbk[HC:], heads)
    dbe = dbi * f["down"] + dbf * f["fade"]
    ends = dbf * f["bf"] + dkf * f["kf"]
    dbefore = dal * f["al"]
    dcum = drs * f["rs"] - dbi * f["bi"] - dki * f["ki"] - ends + dbefore
    dtotal = jnp.sum(ends, 0, keepdims=True) + jnp.sum(S * G, 0, keepdims=True) * f["decay"]
    row, col = iotas(CHUNK, CHUNK)
    upper = ones_where(row <= col)
    top = rounded(dcum)
    dr = drs * f["up"]
    dw = mm(upper, top) + mm(upper, dcum - top) + dtotal - dbefore
    dk = dki * f["down"] + dkf * f["fade"]
    dkk = dbe * a - dal * f["ahead"]
    da = dbe * kk

    head_ones = heads_mask(heads, HEAD).astype(BF)

    def head_sum(value):
        value_top = value.astype(BF)
        rest = (value - value_top.astype(F32)).astype(BF)
        return product(value_top, head_ones) + product(rest, head_ones)

    key_gain, scale_gain, bonus = lines_ref[0:1], lines_ref[1:2], lines_ref[2:3]
    key_proj, value_proj = key_ref[...], value_ref[...]
    key_raw = key_proj * key_gain
    inv_norm = lax.rsqrt(head_sum(key_raw * key_raw) / HEAD + 1e-05) / math.sqrt(HEAD)
    key_scale = 1.0 + (a - 1.0) * scale_gain
    seed = head_sum(dout * v)
    extra = head_sum(r * k * bonus)
    grad_k = rounded(dk + seed * r * bonus)
    grad_v = rounded(dv + extra * dout)
    grad_kk = rounded(dkk)
    grad_rate = rounded(da + grad_k * key_proj * scale_gain)
    inner = head_sum(grad_kk * key_raw) / HEAD
    grad_key_raw = inv_norm * (grad_kk - key_raw * inv_norm * inv_norm * HEAD * inner)
    lora = [
        rounded(dw) * decay_slope_ref[...],
        grad_rate * rate_slope_ref[...],
        rounded(grad_v * (first - value_proj)) * gate_slope_ref[...],
    ]
    proj_grads = (
        (dr + seed * k * bonus).astype(BF),
        (grad_k * key_scale + grad_key_raw * key_gain).astype(BF),
        (grad_v * (1.0 - mix)).astype(BF),
    )
    for ref, value in zip((receptance_out, key_out, value_out), proj_grads):
        ref[...] = value
    lora_all = jnp.concatenate([x.astype(BF) for x in lora] + [out_grad_ref[...]], 1)
    lora_out[...] = lora_all
    token_out[...] = jnp.concatenate(
        [product(lora_all, blocks_ref[...], "nt").astype(BF), (grad_v * mix).astype(BF)], 1
    )
    added = lora + [
        grad_key_raw * key_proj,
        grad_k * key_proj * (a - 1.0),
        seed * r * k,
    ]
    for at, value in enumerate(added):
        sums_ref[at : at + 1] += jnp.sum(value, 0, keepdims=True)

    delta = delta_ref[...]
    straight = jnp.zeros(delta.shape, F32)
    shift = jnp.zeros(delta.shape, F32)
    for i, (grad, source) in enumerate(zip(proj_grads, (0, 2, 3))):
        back = product(grad, weight_ref[:, i * W : (i + 1) * W], "nt")
        part = back * mix_ref[source : source + 1]
        shift = shift + part
        straight = straight + (back - part)
        mix_sums_ref[i : i + 1] += jnp.sum(back * delta, 0, keepdims=True)
    chunk = pl.num_programs(0) - 1 - pl.program_id(0)
    tokens = per_block * CHUNK
    at = pl.multiple_of(lax.rem(chunk, jnp.int32(per_block)) * CHUNK, CHUNK)
    back_ref[0, pl.ds(at, CHUNK)] = (straight + shift_up(shift, behind[0:1])).astype(BF)
    row = lax.broadcasted_iota(jnp.int32, (EDGE, shift.shape[1]), 0)
    edge = jnp.where((row == 0) & (chunk == 0), shift[0:1], 0.0)
    back_ref[0, tokens:] = edge.astype(BF)
    behind[0:1] = shift[0:1]


EDGE = 16


def run_backward(chunk_arrays, delta, starts, tri, enter, end, lines, blocks_out, weights, mix, tokens):
    span, W = chunk_arrays[0].shape
    D = delta.shape[1]
    heads, count = W // HEAD, span // CHUNK
    HC = heads * CHUNK
    per_block = tokens // CHUNK
    flat = jax.ShapeDtypeStruct((span, W), BF)
    return pl.pallas_call(
        functools.partial(backward_kernel, heads, per_block),
        grid=(count,),
        in_specs=[chunk_spec(W, count, True)] * len(chunk_arrays)
        + [
            chunk_spec(D, count, True),
            stack_spec((2 * W, W), count, True),
            stack_spec((HC, HC), count, True),
            whole_spec((W, W)),
            whole_spec((W, W)),
            whole_spec((8, W)),
            whole_spec(blocks_out.shape),
            whole_spec(weights.shape),
            whole_spec(mix.shape),
        ],
        out_specs=[chunk_spec(W, count, True)] * 3
        + [
            chunk_spec(4 * W, count, True),
            chunk_spec(blocks_out.shape[0] + W, count, True),
            whole_spec((8, W)),
            pl.BlockSpec(
                (1, tokens + EDGE, D),
                lambda i: (lax.div(count - 1 - i, jnp.int32(per_block)), 0, 0),
            ),
            whole_spec((8, D)),
        ],
        out_shape=[flat] * 3
        + [
            jax.ShapeDtypeStruct((span, 4 * W), BF),
            jax.ShapeDtypeStruct((span, blocks_out.shape[0] + W), BF),
            jax.ShapeDtypeStruct((8, W), F32),
            jax.ShapeDtypeStruct((span // tokens, tokens + EDGE, D), BF),
            jax.ShapeDtypeStruct((8, D), F32),
        ],
        scratch_shapes=[pltpu.VMEM((W, W), F32), pltpu.VMEM((8, D), F32)],
        compiler_params=pltpu.CompilerParams(vmem_limit_bytes=60 * 1024 * 1024),
        cost_estimate=pl.CostEstimate(
            flops=count * 42 * 2 * HC * HC * W, bytes_accessed=count * 2**20, transcendentals=0
        ),
        name="recurrence_backward",
    )(*chunk_arrays, delta, starts, tri, enter, end, lines, blocks_out, weights, mix)


def widen(narrow, mask):
    heads = mask.shape[0] // HEAD
    return jnp.concatenate([narrow] * heads, 1) * mask


def enter_kernel(heads, place_ref, maps_ref, out_ref):
    mask = heads_mask(heads, HEAD)

    def step(j, carried):
        both = maps_ref[j].astype(F32)
        return fine(carried, widen(both[:, HEAD:], mask)) + widen(both[:, :HEAD], mask)

    out_ref[...] = lax.fori_loop(0, place_ref[0], step, jnp.zeros(out_ref.shape, F32))


def leave_kernel(heads, place_ref, maps_ref, offsets_ref, out_ref):
    mask = heads_mask(heads, HEAD)
    spans = maps_ref.shape[0]

    def step(i, carried):
        j = spans - 1 - i
        linear = widen(maps_ref[j].astype(F32)[:, HEAD:], mask)
        return fine(linear, carried) + jnp.concatenate(
            [offsets_ref[j].astype(F32)] * heads, 0
        ) * mask

    out_ref[...] = lax.fori_loop(
        0, spans - 1 - place_ref[0], step, jnp.zeros(out_ref.shape, F32)
    ).T


def run_chain(kernel, place, *arrays):
    W = arrays[0].shape[1]
    return pl.pallas_call(
        functools.partial(kernel, W // HEAD),
        in_specs=[pl.BlockSpec(memory_space=pltpu.SMEM)]
        + [pl.BlockSpec(memory_space=pltpu.VMEM)] * len(arrays),
        out_specs=pl.BlockSpec(memory_space=pltpu.VMEM),
        out_shape=jax.ShapeDtypeStruct((W, W), F32),
        compiler_params=pltpu.CompilerParams(vmem_limit_bytes=60 * 1024 * 1024),
        name=kernel.__name__,
    )(place.reshape(1).astype(jnp.int32), *arrays)


VMEM_LIMIT = pltpu.CompilerParams(vmem_limit_bytes=60 * 1024 * 1024)


def lowrank_kernel(
    cuts, place_ref, came_ref, slope_ref, in_ref, m1, m4, m3, m5, delta_ref, mix_ref,
    low_ref, sums_ref, straight_ref, shift_ref,
):
    ranks = slope_ref.shape[1]
    total = came_ref[0, :, :ranks].astype(F32)
    for i in range(1, came_ref.shape[0]):
        total = total + came_ref[i, :, :ranks].astype(F32)
    grads = total * slope_ref[...]
    lane = lax.broadcasted_iota(jnp.int32, grads.shape, 1)
    delta = delta_ref[...]
    full_in = in_ref[:, in_ref.shape[1] - ranks :]
    sums_ref[...] = jnp.zeros(sums_ref.shape, F32)
    low = jnp.zeros(low_ref.shape, F32)
    straight = jnp.zeros(delta.shape, F32)
    shift = jnp.zeros(delta.shape, F32)
    for i, ((lo, hi), ref, source) in enumerate(zip(cuts, (m1, m4, m3, m5), (1, 4, 3, 5))):
        part_grads = jnp.where((lane >= lo) & (lane < hi), grads, 0.0).astype(BF)
        low = low + product(part_grads, ref[...], "tn")
        back = product(part_grads, full_in, "nt")
        part = back * mix_ref[source : source + 1]
        shift = shift + part
        straight = straight + (back - part)
        sums_ref[i : i + 1] = jnp.sum(back * delta, 0, keepdims=True)
    low_ref[...] = low
    straight_ref[...] = straight
    shift_ref[...] = shift


def run_lowrank(place, came, slope, by_rows, mixed, delta, mix, cuts):
    groups, tokens, _ = came.shape
    ranks = slope.shape[1]
    D = by_rows.shape[0]

    def fixed(shape):
        return pl.BlockSpec(shape, lambda i, at: (0,) * len(shape))

    def own_block(width):
        return pl.BlockSpec((tokens, width), lambda i, at: (at[0], 0))

    return pl.pallas_call(
        functools.partial(lowrank_kernel, cuts),
        grid_spec=pltpu.PrefetchScalarGridSpec(
            num_scalar_prefetch=1,
            grid=(1,),
            in_specs=[fixed(came.shape), own_block(ranks), fixed(by_rows.shape)]
            + [own_block(D)] * 5
            + [fixed(mix.shape)],
            out_specs=[fixed((ranks, D)), fixed((8, D)), fixed((tokens, D)), fixed((tokens, D))],
        ),
        out_shape=[
            jax.ShapeDtypeStruct((ranks, D), F32),
            jax.ShapeDtypeStruct((8, D), F32),
            jax.ShapeDtypeStruct((tokens, D), F32),
            jax.ShapeDtypeStruct((tokens, D), F32),
        ],
        compiler_params=VMEM_LIMIT,
        cost_estimate=pl.CostEstimate(
            flops=16 * tokens * ranks * D, bytes_accessed=24 * tokens * D, transcendentals=0
        ),
        name="lowrank_back",
    )(place.reshape(1).astype(jnp.int32), came, slope, by_rows, *mixed, delta, mix)


def finish_kernel(
    place_ref, came_ref, straight_ref, shift_ref, behind_ref, normal_ref, inv_ref, resid_ref,
    lines_ref, out_ref, sums_ref,
):
    tokens = straight_ref.shape[0]
    grad = straight_ref[...] + shift_up(shift_ref[...], behind_ref[...])
    for i in range(came_ref.shape[0]):
        grad = grad + came_ref[i, :tokens].astype(F32)
    normal = normal_ref[...]
    scaled = grad * lines_ref[0:1]
    sums_ref[...] = jnp.zeros(sums_ref.shape, F32)
    sums_ref[0:1] = jnp.sum(grad * normal, 0, keepdims=True)
    sums_ref[1:2] = jnp.sum(grad, 0, keepdims=True)
    out_ref[...] = resid_ref[...] + inv_ref[...] * (
        scaled
        - jnp.mean(scaled, -1, keepdims=True)
        - normal * jnp.mean(scaled * normal, -1, keepdims=True)
    )


def run_finish(place, came, straight, shift, behind, normal, inv, resid, lines):
    tokens, D = straight.shape

    def fixed(shape):
        return pl.BlockSpec(shape, lambda i, at: (0,) * len(shape))

    def own_block(width):
        return pl.BlockSpec((tokens, width), lambda i, at: (at[0], 0))

    return pl.pallas_call(
        finish_kernel,
        grid_spec=pltpu.PrefetchScalarGridSpec(
            num_scalar_prefetch=1,
            grid=(1,),
            in_specs=[
                fixed(came.shape),
                fixed((tokens, D)),
                fixed((tokens, D)),
                fixed((1, D)),
                own_block(D),
                own_block(1),
                fixed((tokens, D)),
                fixed(lines.shape),
            ],
            out_specs=[fixed((tokens, D)), fixed((8, D))],
        ),
        out_shape=[
            jax.ShapeDtypeStruct((tokens, D), F32),
            jax.ShapeDtypeStruct((8, D), F32),
        ],
        compiler_params=VMEM_LIMIT,
        cost_estimate=pl.CostEstimate(
            flops=16 * tokens * D, bytes_accessed=30 * tokens * D, transcendentals=0
        ),
        name="norm_back",
    )(place.reshape(1).astype(jnp.int32), came, straight, shift, behind, normal, inv, resid, lines)


def pack_kernel(
    cuts, m0, m2, m3, r_ref, k_ref, v_ref, hid_ref, lora_ref, sums_ref, out_ref
):
    spans, tall, _ = out_ref.shape
    D, W = m0.shape[1], r_ref.shape[1]
    rows = D // spans
    share, room = W // spans, tall - rows
    out_ref[...] = jnp.zeros(out_ref.shape, BF)
    for i, (tokens_ref, grad) in enumerate(((m0, r_ref), (m2, k_ref), (m3, v_ref))):
        whole = product(tokens_ref[...], grad[...], "tn").astype(BF)
        for j in range(spans):
            out_ref[j, :rows, i * W : (i + 1) * W] = whole[j * rows : (j + 1) * rows]
    hid = hid_ref[...]
    ranks = hid.shape[1]
    lane = lax.broadcasted_iota(jnp.int32, hid.shape, 1)
    total = jnp.zeros((W, ranks), F32)
    for i, (lo, hi) in enumerate(cuts):
        part = jnp.where((lane >= lo) & (lane < hi), hid, 0).astype(BF)
        total = total + product(lora_ref[:, i * W : (i + 1) * W], part, "tn")
    total = total.astype(BF)
    sums = sums_ref[...].astype(BF)
    row, col = iotas(room, W)
    for j in range(spans):
        pick = ones_where((col == row + j * share) & (row < share)).astype(BF)
        out_ref[j, rows:, :ranks] = product(pick, total).astype(BF)
        out_ref[j, rows:, ranks : ranks + sums.shape[0]] = product(pick, sums, "nt").astype(BF)


def run_pack(mixed, proj_grads, hid, lora_grads, sums, cuts, spans):
    span, D = mixed[0].shape
    W = proj_grads[0].shape[1]
    columns = hid.shape[1] + sums.shape[0]
    room = -(-(W // spans) // 16) * 16
    return pl.pallas_call(
        functools.partial(pack_kernel, cuts),
        out_shape=jax.ShapeDtypeStruct((spans, D // spans + room, max(3 * W, columns)), BF),
        compiler_params=VMEM_LIMIT,
        cost_estimate=pl.CostEstimate(
            flops=6 * span * W * D, bytes_accessed=8 * span * D, transcendentals=0
        ),
        name="projections_weights",
    )(*mixed, *proj_grads, hid, lora_grads, sums)


def channel_kernel(
    rows_ref, cot_ref, key_ref, value_ref, pre_ref, squared_ref, back_ref, out_ref, back, out
):
    @pl.when(pl.program_id(0) == 0)
    def _():
        back[...] = jnp.zeros(back.shape, F32)
        out[...] = jnp.zeros(out.shape, F32)

    key, value = key_ref[...], value_ref[...]
    active = jnp.maximum(product(rows_ref[...], key), 0.0)
    grad_pre = (product(cot_ref[...], value) * 2.0 * active).astype(BF)
    squared = (active * active).astype(BF)
    pre_ref[...] = grad_pre
    squared_ref[...] = squared
    back[...] += product(grad_pre, key, "nt")
    out[...] += product(squared, value, "nt")

    @pl.when(pl.program_id(0) == pl.num_programs(0) - 1)
    def _():
        back_ref[...] = back[...].astype(BF)
        out_ref[...] = out[...].astype(BF)


def run_channel(rows, cot, key, value):
    span, D = rows.shape
    units = value.shape[1]
    width = min(units, 256)
    return pl.pallas_call(
        channel_kernel,
        grid=(units // width,),
        in_specs=[whole_spec((span, D))] * 2
        + [pl.BlockSpec((D, width), lambda i: (0, i))] * 2,
        out_specs=[pl.BlockSpec((span, width), lambda i: (0, i))] * 2
        + [whole_spec((span, D))] * 2,
        out_shape=[jax.ShapeDtypeStruct((span, units), BF)] * 2
        + [jax.ShapeDtypeStruct((span, D), BF)] * 2,
        scratch_shapes=[pltpu.VMEM((span, D), F32)] * 2,
        compiler_params=VMEM_LIMIT,
        cost_estimate=pl.CostEstimate(
            flops=8 * span * D * units, bytes_accessed=8 * span * D, transcendentals=0
        ),
        name="channel_mix",
    )(rows, cot, key, value)


def value_kernel(cot_ref, squared_ref, grad_ref, att_ref, out_ref):
    units = squared_ref.shape[1]
    out_ref[:, :units] = product(cot_ref[...], squared_ref[...], "tn").astype(BF)
    out_ref[:, units:] = product(grad_ref[...], att_ref[...], "tn").astype(BF)


def run_value(cot, squared, grad_att, att):
    span, D = cot.shape
    units, W = squared.shape[1], att.shape[1]
    width = min(D, 256)
    return pl.pallas_call(
        value_kernel,
        grid=(D // width,),
        in_specs=[
            pl.BlockSpec((span, width), lambda i: (0, i)),
            whole_spec((span, units)),
            pl.BlockSpec((span, width), lambda i: (0, i)),
            whole_spec((span, W)),
        ],
        out_specs=pl.BlockSpec((width, units + W), lambda i: (i, 0)),
        out_shape=jax.ShapeDtypeStruct((D, units + W), BF),
        compiler_params=VMEM_LIMIT,
        cost_estimate=pl.CostEstimate(
            flops=2 * span * D * (units + W), bytes_accessed=8 * span * D, transcendentals=0
        ),
        name="value_weights",
    )(cot, squared, grad_att, att)


def swap(block, axis, bit):
    return lax.ppermute(block, axis, [(i, i ^ bit) for i in range(lax.axis_size(axis))])


def pieces_of(block, axis):
    place = lax.axis_index(axis)
    return [(place, block)] + [
        (place ^ bit, swap(block, axis, bit)) for bit in range(1, lax.axis_size(axis))
    ]


def gather_rows(block, axis):
    count = lax.axis_size(axis)
    whole = jnp.zeros((count,) + block.shape, block.dtype)
    for index, piece in pieces_of(block, axis):
        whole = lax.dynamic_update_index_in_dim(whole, piece, index, 0)
    return whole.reshape((count * block.shape[0],) + block.shape[1:])


def exchange(blocks, axis):
    return lax.all_to_all(blocks, axis, split_axis=0, concat_axis=0, tiled=True)


def hand_round(block, axis):
    count = lax.axis_size(axis)
    copies = jnp.broadcast_to(block[None], (count,) + block.shape)
    return exchange(copies, axis).reshape((count * block.shape[0],) + block.shape[1:])


def scatter_sum(partial, axis):
    count = lax.axis_size(axis)
    blocks = partial.reshape((count, partial.shape[0] // count) + partial.shape[1:])
    return jnp.sum(exchange(blocks, axis).astype(F32), 0)


def after(value, *earlier):
    return lax.optimization_barrier((value,) + earlier)[0]


def moved(block, axis, distance):
    devices = range(lax.axis_size(axis))
    route = [(i - distance, i) for i in devices if i - distance in devices]
    return lax.ppermute(block, axis, route)


def normalize(hidden):
    centered = hidden - jnp.mean(hidden, -1, keepdims=True)
    inv_std = lax.rsqrt(jnp.mean(centered * centered, -1, keepdims=True) + 1e-05)
    return centered * inv_std, inv_std


def norm_grad(grad_out, normal, inv_std, gain_row):
    scaled = grad_out * gain_row
    grad_in = inv_std * (
        scaled
        - jnp.mean(scaled, -1, keepdims=True)
        - normal * jnp.mean(scaled * normal, -1, keepdims=True)
    )
    return grad_in, jnp.sum(grad_out * normal, 0), jnp.sum(grad_out, 0)


def local(
    layer_input_rows,
    first_layer_values,
    cotangent,
    projection_weights,
    output_weight,
    lowrank_in_factors,
    lowrank_out_factors,
    shift_mix_factors,
    parameter_lines,
    channel_key_weight,
    channel_value_weight,
):
    tokens, D = layer_input_rows.shape
    spans, groups = lax.axis_size("ctx"), lax.axis_size("hd")
    ctx, hd = lax.axis_index("ctx"), lax.axis_index("hd")
    span = tokens * groups
    W = projection_weights.shape[2]
    heads = W // HEAD
    ranks = lowrank_in_factors.shape[1]
    own_row = hd * tokens

    def own(rows):
        return lax.dynamic_slice_in_dim(rows, own_row, tokens, 0)

    row_copies = jnp.broadcast_to(layer_input_rows[None], (groups, tokens, D))
    by_columns = lax.all_gather(
        after(
            jnp.concatenate([lowrank_out_factors, shift_mix_factors, parameter_lines], 0),
            row_copies,
        ),
        "ctx",
        axis=0,
        tiled=False,
    )
    by_rows = lax.all_gather(
        jnp.concatenate([projection_weights[i] for i in range(3)] + [lowrank_in_factors], 1),
        "ctx",
        axis=0,
        tiled=True,
    )

    def laid_out(start, rows):
        return by_columns[:, start : start + rows].transpose(1, 0, 2).reshape(rows, D)

    group_proj = by_rows[:, : 3 * W]
    full_in = by_rows[:, 3 * W :]
    rows_span = exchange(row_copies, "hd").reshape(span, D)
    first_span = exchange(
        first_layer_values.reshape(tokens, groups, W).transpose(1, 0, 2), "hd"
    ).reshape(span, W)
    key_matrix = lax.all_gather(after(channel_key_weight, by_rows), "ctx", axis=0, tiled=True)

    token_mixing = laid_out(ranks, 7).astype(F32)
    mix_rows = jnp.concatenate([token_mixing, jnp.zeros((1, D), F32)], 0)
    lines = laid_out(ranks + 7, 12).astype(F32)
    b1, b2, b3 = DECAY_LOWRANK, DECAY_LOWRANK + RA, DECAY_LOWRANK + RA + RV
    cuts = ((0, b1), (b1, b2), (b2, b3), (b3, ranks))
    group_lines = lax.dynamic_slice_in_dim(lines, hd * W, W, 1)
    group_out = lax.dynamic_slice_in_dim(laid_out(0, ranks), hd * W, W, 1)
    out_row = lax.broadcasted_iota(jnp.int32, (ranks, W), 0)
    blocks_out = jnp.concatenate(
        [
            jnp.where((out_row >= lo) & (out_row < hi), group_out, 0).astype(BF)
            for lo, hi in cuts
        ],
        1,
    )

    edge = moved(rows_span[-1:], "ctx", 1).astype(F32)
    hidden = rows_span.astype(F32)
    normal_one, inv_one = normalize(hidden)
    normed = normal_one * lines[0] + lines[1]
    edge_normed = jnp.where(ctx == 0, 0.0, normalize(edge)[0] * lines[0] + lines[1])
    delta_one = jnp.concatenate([edge_normed, normed[:-1]], 0) - normed
    mixed = [(normed + delta_one * token_mixing[i]).astype(BF) for i in range(6)]

    out_rows = gather_rows(after(output_weight.T, mixed[0]), "hd")
    out_rows = out_rows.reshape(groups, D // spans, W).transpose(1, 0, 2).reshape(D // spans, D)
    out_turned = lax.all_gather(out_rows, "ctx", axis=0, tiled=True)
    out_group = lax.dynamic_slice_in_dim(out_turned, hd * W, W, 1)
    receptance = product(mixed[0], group_proj[:, :W])
    key_proj = product(mixed[2], group_proj[:, W : 2 * W])
    value_proj = product(mixed[3], group_proj[:, 2 * W :])

    sources = (1, 4, 3, 5)
    in_column = lax.broadcasted_iota(jnp.int32, full_in.shape, 1)
    pre = jnp.zeros((span, ranks), F32)
    for s, (lo, hi) in zip(sources, cuts):
        part = jnp.where((in_column >= lo) & (in_column < hi), full_in, 0).astype(BF)
        pre = pre + product(mixed[s], part)
    hid_column = lax.broadcasted_iota(jnp.int32, pre.shape, 1)
    tanh_pre, sig_pre = jnp.tanh(pre), jax.nn.sigmoid(pre)
    hid = jnp.where(
        hid_column < b1, tanh_pre, jnp.where(hid_column < b3, pre, sig_pre)
    ).astype(BF)
    hid_slope = jnp.where(
        hid_column < b1,
        1.0 - tanh_pre * tanh_pre,
        jnp.where(hid_column < b3, 1.0, sig_pre * (1.0 - sig_pre)),
    )
    lora_all = product(hid, blocks_out)
    lora = [lora_all[:, i * W : (i + 1) * W] for i in range(4)]
    decay_arg = group_lines[6] + lora[0]
    decay_log = -jnp.exp(-jax.nn.softplus(-decay_arg) - 0.5)
    rate = jax.nn.sigmoid(group_lines[7] + lora[1])
    value_gate = jax.nn.sigmoid(group_lines[8] + lora[2])
    decay_s, rate_s, value_gate_s, gate_s = [
        x.astype(BF) for x in (decay_log, rate, value_gate, lora[3])
    ]
    rate_f, mix_f, gate_f = [x.astype(F32) for x in (rate_s, value_gate_s, gate_s)]
    first_f = first_span.astype(F32)

    head_ones = heads_mask(heads, HEAD)

    def head_sum(value):
        return exact(value, head_ones)

    _, _, group_gain, group_bias, _, _, _, _, _, key_gain, scale_gain, bonus = [
        group_lines[i] for i in range(12)
    ]
    key_raw = key_proj * key_gain
    inv_norm = lax.rsqrt(head_sum(key_raw * key_raw) / HEAD + 1e-05) / math.sqrt(HEAD)
    key_scale = 1.0 + (rate_f - 1.0) * scale_gain
    r_s = receptance.astype(BF)
    k_s = (key_proj * key_scale).astype(BF)
    v_s = (value_proj + (first_f - value_proj) * mix_f).astype(BF)
    kk_s = (key_raw * inv_norm).astype(BF)
    r_f, k_f, v_f = [x.astype(F32) for x in (r_s, k_s, v_s)]

    y_both, starts, tri, last = run_forward(
        r_s, decay_s, k_s, v_s, kk_s, rate_s
    )
    maps = hand_round(last.astype(BF), "ctx").reshape(spans, W, 2 * HEAD)
    value_turned = lax.all_gather(
        after(channel_value_weight.T, by_rows, out_rows), "ctx", axis=0, tiled=True
    )
    cot_span = hand_round(after(cotangent, r_s), "hd")
    enter = run_chain(enter_kernel, ctx, after(maps, cot_span))
    y_reach = y_both[:, W:].astype(BF)
    head_y = y_both[:, :W] + mm(y_reach, enter, "nt")

    head_centered = head_y - head_sum(head_y) / HEAD
    head_inv = lax.rsqrt(head_sum(head_centered * head_centered) / HEAD + 1e-05 * HEAD)
    standard = head_centered * head_inv
    extra = head_sum(r_f * k_f * bonus)
    head_out = rounded(standard * group_gain + group_bias + extra * v_f)
    att = (head_out * gate_f).astype(BF)

    att_out = jnp.zeros((span, D), F32)
    for index, piece in pieces_of(att, "hd"):
        weight = lax.dynamic_slice_in_dim(out_turned, index * W, W, 1)
        att_out = att_out + product(piece, weight, "nt")
    residual = hidden + att_out
    normal_two, inv_two = normalize(residual)
    normed_two = normal_two * lines[4] + lines[5]
    edge_two = moved(normed_two[-1:], "ctx", 1)
    delta_two = jnp.concatenate([edge_two, normed_two[:-1]], 0) - normed_two
    mixed_ffn = (normed_two + delta_two * token_mixing[6]).astype(BF)

    grad_pre, squared, back_part, ffn_part = run_channel(
        mixed_ffn, cot_span, key_matrix, value_turned
    )
    grad_mixed_ffn = scatter_sum(back_part, "hd")

    def over_spans(partial):
        return lax.psum_scatter(partial, "ctx", scatter_dimension=0, tiled=True)

    grad_ffn_key = over_spans(product(mixed_ffn, grad_pre, "tn").astype(BF))

    grad_mix_six = jnp.sum(grad_mixed_ffn * own(delta_two), 0)
    grad_shift_two = grad_mixed_ffn * token_mixing[6]
    behind_two = moved(grad_shift_two[:1], ("ctx", "hd"), -1)
    grad_normed_two = (
        grad_mixed_ffn
        - grad_shift_two
        + jnp.concatenate([grad_shift_two[1:], behind_two], 0)
    )
    grad_resid_norm, grad_gain_two, grad_bias_two = norm_grad(
        grad_normed_two, own(normal_two), own(inv_two), lines[4]
    )
    grad_residual = cotangent.astype(F32) + grad_resid_norm
    grad_att = hand_round(grad_residual.astype(BF), "hd")
    grad_att_in = product(grad_att, out_group)

    adjoint = rounded(grad_att_in * gate_f)
    grad_gate = (grad_att_in * head_out).astype(BF)
    grad_group_gain = jnp.sum(adjoint * standard, 0)
    grad_group_bias = jnp.sum(adjoint, 0)
    scaled = adjoint * group_gain
    grad_head_y = head_inv * (
        scaled - head_sum(scaled) / HEAD - standard * (head_sum(scaled * standard) / HEAD)
    )
    offset_wide = mm(y_reach, grad_head_y, "tn") * head_ones
    offset = fold(offset_wide, heads)
    offsets = hand_round(offset.astype(BF), "ctx").reshape(spans, HEAD, W)
    end = run_chain(leave_kernel, ctx, maps, offsets)
    end, value_part, ffn_part = lax.optimization_barrier(
        (
            end,
            run_value(cot_span, squared, grad_att, att),
            ffn_part,
        )
    )
    value_and_out = over_spans(after(value_part, grad_ffn_key))
    hidden_units = squared.shape[1]
    grad_ffn_value, grad_out = value_and_out[:, :hidden_units], value_and_out[:, hidden_units:]
    ffn_sum = scatter_sum(ffn_part, "hd")
    layer_output = (own(residual) + ffn_sum).astype(BF)
    decay_slope = decay_log * jax.nn.sigmoid(-decay_arg)
    rate_slope = rate * (1.0 - rate)
    gate_slope = value_gate * (1.0 - value_gate)
    own_lines = jnp.concatenate(
        [group_lines[9:12], jnp.zeros((5, W), F32)], 0
    )
    chunk_arrays = (r_s, decay_s, k_s, v_s, kk_s, rate_s, value_gate_s, first_span)
    chunk_arrays += (adjoint.astype(BF), grad_head_y, key_proj, value_proj)
    chunk_arrays += (decay_slope, rate_slope, gate_slope, grad_gate)
    blocks_tall = jnp.pad(blocks_out, ((0, -ranks % 128), (0, 0)))
    *proj_grads, lora_grads, to_tokens, group_sums, back_sum, back_sums = run_backward(
        chunk_arrays,
        delta_one,
        starts,
        tri,
        enter,
        end,
        own_lines,
        blocks_tall,
        by_rows,
        mix_rows,
        tokens,
    )

    to_tokens = exchange(
        after(to_tokens, ffn_sum).reshape(groups, tokens, to_tokens.shape[1]), "hd"
    )
    grad_value_first = (
        to_tokens[:, :, blocks_tall.shape[0] :]
        .transpose(1, 0, 2)
        .reshape(tokens, D)
        .astype(F32)
    )

    def rows_of(vectors):
        row = lax.broadcasted_iota(jnp.int32, (8, vectors[0].shape[-1]), 0)
        out = jnp.zeros(row.shape, F32)
        for i, vector in enumerate(vectors):
            out = jnp.where(row == i, vector.reshape(1, -1), out)
        return out

    proj_grads = [after(proj_grads[0], ffn_sum)] + proj_grads[1:]
    packed = run_pack(
        [mixed[s] for s in (0, 2, 3)],
        proj_grads,
        hid,
        lora_grads,
        jnp.concatenate([group_sums, rows_of([grad_group_gain, grad_group_bias])], 0),
        cuts,
        spans,
    )
    back_sum = exchange(after(back_sum, to_tokens, packed), "hd")
    packed = lax.psum_scatter(
        after(packed, value_and_out), "ctx", scatter_dimension=0, tiled=True
    )[0]
    grad_low, low_sums, straight, shift = run_lowrank(
        hd, to_tokens, hid_slope, by_rows, [mixed[s] for s in sources], delta_one, mix_rows, cuts
    )
    edge_grad = shift[:1] + jnp.where(
        hd == 0, jnp.sum(back_sum[:, tokens : tokens + 1].astype(F32), 0), 0.0
    )
    behind = moved(edge_grad, ("ctx", "hd"), -1)
    grad_input, norm_sums = run_finish(
        hd, back_sum, straight, shift, behind, normal_one, inv_one, grad_residual, lines
    )
    grad_proj = packed[: D // spans, : 3 * W].astype(F32)
    route = [(c * groups + h, h * spans + c) for c in range(spans) for h in range(groups)]
    narrow = lax.ppermute(
        packed[D // spans : D // spans + W // spans, : ranks + 16], ("ctx", "hd"), route
    ).astype(F32)

    wide = jnp.concatenate(
        [
            grad_low,
            back_sums,
            low_sums,
            norm_sums,
            rows_of([grad_mix_six, grad_gain_two, grad_bias_two]),
        ],
        0,
    ).astype(BF)
    by_owner = wide.T.reshape(spans, groups, D // spans // groups, wide.shape[0])
    over_hd = jnp.sum(exchange(by_owner.transpose(1, 0, 2, 3), "hd").astype(F32), 0)
    over_ctx = exchange(over_hd.astype(BF), "ctx")
    wide = jnp.sum(after(over_ctx, narrow).astype(F32), 0)

    grad_lora_in = wide[:, :ranks]
    rows = wide[:, ranks:].T
    mix_three = rows[2:3] + rows[10:11]
    grad_mix_coef = jnp.concatenate(
        [rows[0:2], mix_three, rows[9:10], rows[11:12], rows[24:25]], 0
    )
    group_part = narrow[:, :ranks].T
    vectors = narrow[:, ranks:].T
    grad_vectors = jnp.concatenate(
        [rows[16:18], vectors[8:10], rows[25:27], vectors[:6]], 0
    )
    return (
        layer_output,
        grad_input,
        grad_value_first,
        grad_proj.reshape(D // spans, 3, W).transpose(1, 0, 2),
        grad_out.astype(F32).T,
        grad_lora_in,
        group_part,
        grad_mix_coef,
        grad_vectors,
        grad_ffn_key.astype(F32),
        grad_ffn_value.astype(F32).T,
        rows[8],
    )


def solution(mesh):
    in_specs = (
        P(("ctx", "hd"), None),
        P(("ctx", "hd"), None),
        P(("ctx", "hd"), None),
        P(None, "ctx", "hd"),
        P("hd", "ctx"),
        P("ctx", None),
        P(None, "ctx"),
        P(None, "ctx"),
        P(None, "ctx"),
        P("ctx", "hd"),
        P("hd", "ctx"),
    )
    out_specs = (
        P(("ctx", "hd"), None),
        P(("ctx", "hd"), None),
        P(("ctx", "hd"), None),
        P(None, "ctx", "hd"),
        P("hd", "ctx"),
        P(("ctx", "hd"), None),
        P(None, ("ctx", "hd")),
        P(None, ("ctx", "hd")),
        P(None, ("ctx", "hd")),
        P("ctx", "hd"),
        P("hd", "ctx"),
        P(("ctx", "hd")),
    )
    return jax.shard_map(local, mesh=mesh, in_specs=in_specs, out_specs=out_specs, check_vma=False)
```
